32 devices in a mesh: grp: 2 (over y), samp: 4 (over z), term: 4 (over x, core).
Axes of the slice: x: 2, y: 2, z: 4, core: 2. Of those that a mesh axis runs over, the one named last changes fastest.
Arguments:
- blocks: float32 [4, 4, 16, 8, 128, 128], P('samp', 'term', 'grp'), parts along dimension 2, may hold values from -0.09375 to 0.09375
- term_index: int32 [4, 4, 16, 8], P('samp', 'term', 'grp'), parts along dimension 2, may hold values from 0 to 63, as said below
- degrees: int32 [256], P('term'), may hold values from 0 to 5, as said below
- targets: float32 [64, 4096], P('grp', 'samp'), parts along dimension 0, may hold values from -6 to 6
Outputs:
- solution: float32 [64, 32768], P('grp', 'term'), parts along dimension 0
- residual: float32 [64, 4096], P('grp', 'samp'), parts along dimension 0
The draws below stay inside these ranges and needn't reach their ends.
There are 2 independent parts, one for each index of `grp`. The reference program is written for one: setup_inputs(seed, part) draws one part's arguments, and reference() takes and returns one part's arrays. A program takes and returns all parts, laid end to end along the dimension named above; an argument that names none is the same for every part. Nothing has to cross between parts.
Inputs may be any that keep to these rules, and one draw needn't show every extreme that they name: `term_index`: each row block holds the gradient rows of one of 40 inputs; on each term device the row blocks of input k touch the 8 term blocks (k * 8 + c + [0, 8)) modulo 64, with c fixed for that term device; so in each row block the indices are distinct. Basis blocks are ordered by total degree: degrees never fall by more than one from a block to a later one.
All inputs are finite; a program needn't handle non-finite values.
Results may differ from the reference program's by a relative error of at most 0.0001.
Values sent between devices are 32-bit elements; how exact they have to be, the bound alone decides.
A program may use at most 64 MiB of HBM per device.

```python
import jax
import jax.numpy as jnp
from jax import lax

BLK = 128
TERMS = 32768
NIN = 40
QOI = 32
RB_DEV = 8
NBR = 8
ITERS = 2
TB_DEV = 64
TBLOCKS = 256
ROWS = 4096
N_SAMP = 4
N_TERM = 4


def draw_term_index(key, part):
    count = N_SAMP * RB_DEV
    rotation = jax.random.randint(jax.random.fold_in(key, 11), (N_TERM,), 0, TB_DEV)
    offset = jax.random.randint(jax.random.fold_in(key, 12), (), 0, NIN)
    shuffled = jax.random.permutation(jax.random.fold_in(key, 13), count)
    which_input = ((offset + shuffled) % NIN).reshape(N_SAMP, RB_DEV)
    steps_in = jnp.arange(NBR, dtype=jnp.int32)
    start = which_input[:, None, :] * NBR + rotation[None, :, None]
    picked = (start[..., None] + steps_in) % TB_DEV
    return picked.astype(jnp.int32)


def draw_degrees(key, part):
    key = jax.random.fold_in(key, 21)
    graded = jnp.arange(TBLOCKS, dtype=jnp.int32) * 5 // TBLOCKS
    jitter = jax.random.randint(key, (TBLOCKS,), 0, 2)
    values = jnp.minimum(graded + jitter, 5)
    values = values.at[0].set(0)
    values = values.at[TBLOCKS - 1].set(5)
    return values.astype(jnp.int32)


def block_levels(key, extent, cuts, least, high):
    loudness = 1.0
    for axis_at, shards_of in cuts:
        steps = jax.random.uniform(jax.random.fold_in(jax.random.fold_in(key, 6), axis_at), (shards_of,), jnp.float32, least / len(cuts), high / len(cuts))
        loudness = loudness * jnp.repeat(jnp.exp(steps), extent[axis_at] // shards_of).reshape((-1,) + (1,) * (len(extent) - 1 - axis_at))
    return loudness


def scatter_about(key, shape, width, bound, split=(), kind=jnp.bfloat16):
    gain = block_levels(key, shape, split, -0.22, 0.18) if split else 1.0
    values = jax.random.normal(key, shape, jnp.float32) * width * gain
    return jnp.minimum(jnp.maximum(values, -bound), bound).astype(kind)


def setup_inputs(seed: int = 0, part: int = 0) -> dict:
    arg_keys = jax.random.split(jax.random.key(seed), 5)
    part_splits = jax.random.split(jax.random.fold_in(arg_keys[4], part), 5)
    return {
        "blocks": scatter_about(part_splits[0], (N_SAMP, N_TERM, RB_DEV, NBR, BLK, BLK), (BLK * NBR * N_TERM) ** -0.5, 0.09375, ((0, 4), (1, 4)), jnp.float32),
        "term_index": draw_term_index(jax.random.fold_in(jax.random.fold_in(arg_keys[4], part), 71), part),
        "degrees": draw_degrees(jax.random.fold_in(arg_keys[4], 71), part),
        "targets": scatter_about(part_splits[3], (QOI, ROWS), 1.0, 6.0, ((1, 4),), jnp.float32),
    }


def forward_all(blocks, onehot, direction):
    num_out = direction.shape[0]
    shaped = direction.reshape(num_out, N_TERM, TB_DEV, BLK)
    picked = jnp.einsum("qjbt,ijrnb->qijrnt", shaped, onehot, precision=lax.Precision.HIGHEST)
    image = jnp.einsum("qijrnt,ijrnxt->qirx", picked, blocks, precision=lax.Precision.HIGHEST)
    return image.reshape(num_out, ROWS)


def adjoint_all(blocks, onehot, residual):
    num_out = residual.shape[0]
    shaped = residual.reshape(num_out, N_SAMP, RB_DEV, BLK)
    partial_terms = jnp.einsum("qirx,ijrnxt->qijrnt", shaped, blocks, precision=lax.Precision.HIGHEST)
    summed = jnp.einsum("qijrnt,ijrnb->qjbt", partial_terms, onehot, precision=lax.Precision.HIGHEST)
    return summed.reshape(num_out, TERMS)


def reference(blocks, term_index, degrees, targets):
    onehot = (term_index[..., None] == jnp.arange(TB_DEV, dtype=jnp.int32)).astype(jnp.float32)
    damping = jnp.repeat(0.4 * (1.0 + degrees.astype(jnp.float32)), BLK)
    solution = jnp.zeros((targets.shape[0], TERMS), jnp.float32)
    residual = targets
    grad = adjoint_all(blocks, onehot, residual)
    direction = grad
    grad_sq = jnp.sum(grad * grad, axis=1)
    for step in range(ITERS):
        image = forward_all(blocks, onehot, direction)
        damped = damping * direction
        curv_sq = jnp.sum(image * image, axis=1) + jnp.sum(damped * damped, axis=1)
        step_size = (grad_sq / curv_sq)[:, None]
        solution = solution + step_size * direction
        residual = residual - step_size * image
        if step + 1 < ITERS:
            grad = adjoint_all(blocks, onehot, residual) - damping * damping * solution
            new_sq = jnp.sum(grad * grad, axis=1)
            direction = grad + (new_sq / grad_sq)[:, None] * direction
            grad_sq = new_sq
    return solution, residual
```

```python
import functools

import jax
import jax.numpy as jnp
from jax import lax
from jax.experimental import pallas as pl
from jax.experimental.pallas import tpu as pltpu
from jax.sharding import PartitionSpec as P

MESH = pl.DeviceIdType.MESH
F32 = jnp.float32
BF16 = jnp.bfloat16


def split(x):
    hi = x.astype(BF16)
    return hi, (x - hi.astype(F32)).astype(BF16)


def lane_sum(x):
    return jnp.sum(x, axis=1, keepdims=True)


def kernel(
    n_samp, n_term, chunks,
    tab, deg, a_ref, t_ref,
    sol_ref, res_ref,
    ahi, alo, part, acc0, acc1, rx0, rx1, d0, w1, g1,
    img0, img1, msg0, msg1, trx0, trx1, sr0, sr1, sq0, sq1,
    in_send, out_send, chain_recv, t_send, t_recv, s_send, s_recv,
):
    rows, touched, width = a_ref.shape[2], a_ref.shape[3], a_ref.shape[4]
    num_out = t_ref.shape[0]
    terms = deg.shape[0]
    size = terms // chunks
    half = n_samp // 2
    rounds = n_term.bit_length() - 1
    me = lax.axis_index("samp")
    tm = lax.axis_index("term")

    low = me < half
    inner = jnp.where(low, me + 1, me - 1)
    is_mid = jnp.logical_or(me == half - 1, me == half)
    has_outer = jnp.logical_and(me > 0, me < n_samp - 1)
    outer = jnp.where(low, jnp.maximum(me - 1, 0), jnp.minimum(me + 1, n_samp - 1))
    slot_at_inner = jnp.where(is_mid, 1, 0)

    def peer_of(off):
        return lax.rem(me + off, n_samp)

    def partner_of(k):
        step = 2 ** k
        return tm + (1 - 2 * lax.rem(tm // step, 2)) * step

    barrier = pltpu.get_barrier_semaphore()

    @pl.loop(1, n_samp)
    def _(off):
        pl.semaphore_signal(barrier, inc=1, device_id={"samp": peer_of(off)}, device_id_type=MESH)

    for k in range(rounds):
        pl.semaphore_signal(barrier, inc=1, device_id={"term": partner_of(k)}, device_id_type=MESH)

    def adjoint(load, first):
        @pl.loop(0, rows)
        def _(r):
            if first:
                for n in range(touched):
                    hi, lo = split(a_ref[0, 0, r, n])
                    ahi[r, :, n * width:(n + 1) * width] = hi
                    alo[r, :, n * width:(n + 1) * width] = lo
                part[r * (touched + 1) + touched] = jnp.zeros((num_out, width), F32)
            hi, lo = split(load(r))
            both = jnp.concatenate([hi, lo], axis=0)
            for n in range(touched):
                cols = slice(n * width, (n + 1) * width)
                p = jnp.dot(both, ahi[r, :, cols], preferred_element_type=F32)
                q = jnp.dot(hi, alo[r, :, cols], preferred_element_type=F32)
                part[r * (touched + 1) + n] = p[:num_out] + p[num_out:] + q

    def forward(src, dst):
        @pl.loop(0, rows)
        def _(r):
            x = jnp.concatenate([src[tab[r, terms + n]] for n in range(touched)], axis=1)
            hi, lo = split(x)
            both = jnp.concatenate([hi, lo], axis=0)
            dims = (((1,), (1,)), ((), ()))
            p = lax.dot_general(both, ahi[r], dims, preferred_element_type=F32)
            q = lax.dot_general(hi, alo[r], dims, preferred_element_type=F32)
            dst[0, r] = p[:num_out] + p[num_out:] + q

    def span(c):
        return pl.ds(c * size, size)

    def to_inner(k, acc, rx, c):
        return pltpu.make_async_remote_copy(
            src_ref=acc.at[span(c)], dst_ref=rx.at[slot_at_inner, span(c)],
            send_sem=in_send.at[k, c], recv_sem=chain_recv.at[k, slot_at_inner, c],
            device_id={"samp": inner}, device_id_type=MESH,
        )

    def to_outer(k, d, rx, c):
        return pltpu.make_async_remote_copy(
            src_ref=d.at[span(c)], dst_ref=rx.at[1, span(c)],
            send_sem=out_send.at[k, c], recv_sem=chain_recv.at[k, 1, c],
            device_id={"samp": outer}, device_id_type=MESH,
        )

    def arrived(k, rx, slot, c):
        pltpu.make_async_remote_copy(
            src_ref=rx.at[slot, span(c)], dst_ref=rx.at[slot, span(c)],
            send_sem=in_send.at[k, c], recv_sem=chain_recv.at[k, slot, c],
            device_id={"samp": inner}, device_id_type=MESH,
        ).wait_recv()

    def chain(k, acc, rx, d, visit, carry):
        def inbound(c):
            @pl.loop(0, size)
            def _(i):
                b = c * size + i
                total = part[tab[0, b]]
                for r in range(1, rows):
                    total = total + part[tab[r, b]]
                acc[b] = total

            @pl.when(has_outer)
            def _():
                arrived(k, rx, 0, c)
                acc[span(c)] += rx[0, span(c)]

            to_inner(k, acc, rx, c).start()

        def outbound(c, carry):
            arrived(k, rx, 1, c)

            def one(i, carry):
                b = c * size + i
                got = rx[1, b]
                v = jnp.where(is_mid, got + acc[b], got)
                d[b] = v
                return visit(b, v, carry)

            carry = lax.fori_loop(0, size, one, carry)

            @pl.when(has_outer)
            def _():
                to_outer(k, d, rx, c).start()

            return carry

        inbound(0)

        def step(c, carry):
            inbound(c)
            return outbound(c - 1, carry)

        carry = lax.fori_loop(1, chunks, step, carry)
        return outbound(chunks - 1, carry)

    def term_copy(s, msg, trx, k):
        return pltpu.make_async_remote_copy(
            src_ref=msg.at[k], dst_ref=trx.at[k],
            send_sem=t_send.at[s, k], recv_sem=t_recv.at[s, k],
            device_id={"term": partner_of(k)}, device_id_type=MESH,
        )

    def term_sum(s, msg, trx):
        for k in range(rounds):
            copy = term_copy(s, msg, trx, k)
            copy.start()
            copy.wait()
            msg[k + 1] = msg[k] + trx[k]

    def sq_copy(s, sq, sr, off):
        return pltpu.make_async_remote_copy(
            src_ref=sq, dst_ref=sr.at[me],
            send_sem=s_send.at[s, off], recv_sem=s_recv.at[s, off],
            device_id={"samp": peer_of(off)}, device_id_type=MESH,
        )

    def samp_start(s, sq, sr):
        @pl.loop(1, n_samp)
        def _(off):
            sq_copy(s, sq, sr, off).start()

        sr[me] = sq[...]

    def samp_finish(s, sq, sr):
        @pl.loop(1, n_samp)
        def _(off):
            sq_copy(s, sq, sr, off).wait()

        total = lax.fori_loop(1, n_samp, lambda i, t: t + sr[i], sr[0])
        return lane_sum(total)

    lane = lax.broadcasted_iota(jnp.int32, (num_out, width), 1)

    def pack(values):
        out = jnp.zeros((num_out, width), F32)
        for at, v in enumerate(values):
            out = jnp.where(lane == at, lane_sum(v), out)
        return out

    def pick(block, at):
        return lane_sum(jnp.where(lane == at, block, 0.0))

    def damp_sq(b):
        d = 0.4 * (1.0 + deg[b].astype(F32))
        return d * d

    zero = jnp.zeros((num_out, width), F32)

    adjoint(lambda r: t_ref[:, pl.ds(pl.multiple_of(r * width, width), width)], True)
    pl.semaphore_wait(barrier, n_samp - 1 + rounds)

    def visit0(b, v, carry):
        gs, os = carry
        sq = v * v
        return gs + sq, os + damp_sq(b) * sq

    gs, os = chain(0, acc0, rx0, d0, visit0, (zero, zero))
    forward(d0, msg0)
    msg0[0, rows] = pack([gs, os])
    term_sum(0, msg0, trx0)
    scal = msg0[rounds, rows]
    gsq0, own0 = pick(scal, 0), pick(scal, 1)

    sq = zero
    for r in range(rows):
        v = msg0[rounds, r]
        img0[r] = v
        sq = sq + v * v
    sq0[...] = sq
    samp_start(0, sq0, sr0)
    adjoint(lambda r: img0[r], False)
    chain(1, acc1, rx1, w1, lambda b, v, c: c, 0)
    alpha0 = gsq0 / (samp_finish(0, sq0, sr0) + own0)
    alpha0 = jnp.broadcast_to(alpha0, (num_out, width))

    def make_grad(b, carry):
        ns, s1, s2 = carry
        dd = damp_sq(b)
        d = d0[b]
        g = d - alpha0 * (w1[b] + dd * d)
        g1[b] = g
        dg = dd * g
        return ns + g * g, s1 + dg * g, s2 + dg * d

    ns, s1, s2 = lax.fori_loop(0, terms, make_grad, (zero, zero, zero))
    forward(g1, msg1)
    msg1[0, rows] = pack([ns, s1, s2])
    term_sum(1, msg1, trx1)
    scal = msg1[rounds, rows]
    gsq1, c1, c2 = pick(scal, 0), pick(scal, 1), pick(scal, 2)
    beta = gsq1 / gsq0
    own1 = c1 + 2.0 * beta * c2 + beta * beta * own0
    beta = jnp.broadcast_to(beta, (num_out, width))

    sq = zero
    for r in range(rows):
        v = msg1[rounds, r] + beta * img0[r]
        img1[r] = v
        sq = sq + v * v
    sq1[...] = sq
    samp_start(1, sq1, sr1)
    alpha1 = gsq1 / (samp_finish(1, sq1, sr1) + own1)
    alpha1 = jnp.broadcast_to(alpha1, (num_out, width))
    both = alpha0 + alpha1 * beta

    @pl.loop(0, terms)
    def _(b):
        sol_ref[:, pl.ds(pl.multiple_of(b * width, width), width)] = both * d0[b] + alpha1 * g1[b]

    for r in range(rows):
        cols = slice(r * width, (r + 1) * width)
        res_ref[:, cols] = t_ref[:, cols] - alpha0 * img0[r] - alpha1 * img1[r]

    for k, (acc, rx, d) in enumerate(((acc0, rx0, d0), (acc1, rx1, w1))):
        @pl.loop(0, chunks)
        def _(c):
            to_inner(k, acc, rx, c).wait_send()

            @pl.when(has_outer)
            def _():
                to_outer(k, d, rx, c).wait_send()


def local(n_samp, n_term, blocks, term_index, degrees, targets):
    rows, touched, width = blocks.shape[2], blocks.shape[3], blocks.shape[4]
    terms = degrees.shape[0]
    num_out = targets.shape[0]
    pattern = term_index[0, 0]
    hit = pattern[:, :, None] == jnp.arange(terms, dtype=jnp.int32)
    at = jnp.arange(touched, dtype=jnp.int32)[None, :, None]
    where = jnp.min(jnp.where(hit, at, touched), axis=1)
    where = where + jnp.arange(rows, dtype=jnp.int32)[:, None] * (touched + 1)
    tab = jnp.concatenate([where, pattern], axis=1)

    chunks = min(16, terms)
    rounds = n_term.bit_length() - 1
    blk = (num_out, width)
    vmem = pl.BlockSpec(memory_space=pltpu.VMEM)
    smem = pl.BlockSpec(memory_space=pltpu.SMEM)
    V = pltpu.VMEM
    dma = pltpu.SemaphoreType.DMA
    return pl.pallas_call(
        functools.partial(kernel, n_samp, n_term, chunks),
        out_shape=(
            jax.ShapeDtypeStruct((num_out, terms * width), F32),
            jax.ShapeDtypeStruct((num_out, rows * width), F32),
        ),
        in_specs=[smem, smem, vmem, vmem],
        out_specs=(vmem, vmem),
        scratch_shapes=[
            V((rows, width, touched * width), BF16),
            V((rows, width, touched * width), BF16),
            V((rows * (touched + 1),) + blk, F32),
            V((terms,) + blk, F32),
            V((terms,) + blk, F32),
            V((2, terms) + blk, F32),
            V((2, terms) + blk, F32),
            V((terms,) + blk, F32),
            V((terms,) + blk, F32),
            V((terms,) + blk, F32),
            V((rows,) + blk, F32),
            V((rows,) + blk, F32),
            V((rounds + 1, rows + 1) + blk, F32),
            V((rounds + 1, rows + 1) + blk, F32),
            V((rounds, rows + 1) + blk, F32),
            V((rounds, rows + 1) + blk, F32),
            V((n_samp,) + blk, F32),
            V((n_samp,) + blk, F32),
            V(blk, F32),
            V(blk, F32),
            dma((2, chunks)),
            dma((2, chunks)),
            dma((2, 2, chunks)),
            dma((2, rounds)),
            dma((2, rounds)),
            dma((2, n_samp)),
            dma((2, n_samp)),
        ],
        compiler_params=pltpu.CompilerParams(
            collective_id=0, has_side_effects=True, vmem_limit_bytes=48 * 1024 * 1024,
        ),
    )(tab, degrees, blocks, targets)


def solution(mesh):
    placed = (
        P("samp", "term", "grp", None, None, None),
        P("samp", "term", "grp", None),
        P("term"),
        P("grp", "samp"),
    )
    return jax.shard_map(
        functools.partial(local, mesh.shape["samp"], mesh.shape["term"]),
        mesh=mesh,
        in_specs=placed,
        out_specs=(P("grp", "term"), P("grp", "samp")),
        check_vma=False,
    )
```

```python
import functools

import jax
import jax.numpy as jnp
from jax import lax
from jax.experimental import pallas as pl
from jax.experimental.pallas import tpu as pltpu
from jax.sharding import PartitionSpec as P

MESH = pl.DeviceIdType.MESH
F32 = jnp.float32
BF16 = jnp.bfloat16
LAG = 3


def split(x):
    hi = x.astype(BF16)
    return hi, (x - hi.astype(F32)).astype(BF16)


def lane_sum(x):
    return jnp.sum(x, axis=1, keepdims=True)


def kernel(
    n_samp, n_term, chunks,
    tab, deg, a_ref, t_ref,
    sol_ref, res_ref,
    ahi, alo, part, acc0, acc1, rx0, rx1, d0, w1, g1,
    img0, img1, msg0, msg1, trx0, trx1, sr0, sr1, sq0, sq1, totals,
    in_send, out_send, chain_recv, t_send, t_recv, s_send, s_recv,
):
    rows, touched, width = a_ref.shape[2], a_ref.shape[3], a_ref.shape[4]
    num_out = t_ref.shape[0]
    terms = deg.shape[0]
    size = terms // chunks
    half = n_samp // 2
    rounds = n_term.bit_length() - 1
    me = lax.axis_index("samp")
    tm = lax.axis_index("term")

    low = me < half
    inner = jnp.where(low, me + 1, me - 1)
    is_mid = jnp.logical_or(me == half - 1, me == half)
    has_outer = jnp.logical_and(me > 0, me < n_samp - 1)
    outer = jnp.where(low, jnp.maximum(me - 1, 0), jnp.minimum(me + 1, n_samp - 1))
    away = jnp.where(low, half - 1 - me, me - half)
    lag = jnp.minimum(LAG * (2 * away + 1), chunks)
    slot_at_inner = jnp.where(is_mid, 1, 0)

    zero = jnp.zeros((num_out, width), F32)

    def peer_of(off):
        return lax.rem(me + off, n_samp)

    def partner_of(k):
        step = 2 ** k
        return tm + (1 - 2 * lax.rem(tm // step, 2)) * step

    barrier = pltpu.get_barrier_semaphore()

    @pl.loop(1, n_samp)
    def _(off):
        pl.semaphore_signal(barrier, inc=1, device_id={"samp": peer_of(off)}, device_id_type=MESH)

    for k in range(rounds):
        pl.semaphore_signal(barrier, inc=1, device_id={"term": partner_of(k)}, device_id_type=MESH)

    def adjoint(load, first):
        @pl.loop(0, rows)
        def _(r):
            if first:
                for n in range(touched):
                    hi, lo = split(a_ref[0, 0, r, n])
                    ahi[r, :, n * width:(n + 1) * width] = hi
                    alo[r, :, n * width:(n + 1) * width] = lo
                part[r * (touched + 1) + touched] = jnp.zeros((num_out, width), F32)
            hi, lo = split(load(r))
            both = jnp.concatenate([hi, lo], axis=0)
            for n in range(touched):
                cols = slice(n * width, (n + 1) * width)
                p = jnp.dot(both, ahi[r, :, cols], preferred_element_type=F32)
                q = jnp.dot(hi, alo[r, :, cols], preferred_element_type=F32)
                part[r * (touched + 1) + n] = p[:num_out] + p[num_out:] + q

    def forward(src, dst):
        @pl.loop(0, rows)
        def _(r):
            x = jnp.concatenate([src[tab[r, terms + n]] for n in range(touched)], axis=1)
            hi, lo = split(x)
            both = jnp.concatenate([hi, lo], axis=0)
            dims = (((1,), (1,)), ((), ()))
            p = lax.dot_general(both, ahi[r], dims, preferred_element_type=F32)
            q = lax.dot_general(hi, alo[r], dims, preferred_element_type=F32)
            dst[0, r] = p[:num_out] + p[num_out:] + q

    def span(c):
        return pl.ds(c * size, size)

    def to_inner(k, acc, rx, c):
        return pltpu.make_async_remote_copy(
            src_ref=acc.at[span(c)], dst_ref=rx.at[slot_at_inner, span(c)],
            send_sem=in_send.at[k, c], recv_sem=chain_recv.at[k, slot_at_inner, c],
            device_id={"samp": inner}, device_id_type=MESH,
        )

    def to_outer(k, d, rx, c):
        return pltpu.make_async_remote_copy(
            src_ref=d.at[span(c)], dst_ref=rx.at[1, span(c)],
            send_sem=out_send.at[k, c], recv_sem=chain_recv.at[k, 1, c],
            device_id={"samp": outer}, device_id_type=MESH,
        )

    def arrived(k, rx, slot, c):
        pltpu.make_async_remote_copy(
            src_ref=rx.at[slot, span(c)], dst_ref=rx.at[slot, span(c)],
            send_sem=in_send.at[k, c], recv_sem=chain_recv.at[k, slot, c],
            device_id={"samp": inner}, device_id_type=MESH,
        ).wait_recv()

    def chain(k, acc, rx, d, visit, sums):
        def inbound(c):
            @pl.loop(0, size)
            def _(i):
                b = c * size + i
                total = part[tab[0, b]]
                for r in range(1, rows):
                    total = total + part[tab[r, b]]
                acc[b] = total

            @pl.when(has_outer)
            def _():
                arrived(k, rx, 0, c)
                acc[span(c)] += rx[0, span(c)]

            to_inner(k, acc, rx, c).start()

        def outbound(c):
            arrived(k, rx, 1, c)

            def one(i, carry):
                b = c * size + i
                got = rx[1, b]
                v = jnp.where(is_mid, got + acc[b], got)
                d[b] = v
                return visit(b, v, carry)

            carry = lax.fori_loop(0, size, one, tuple(zero for _ in range(sums)))
            for at, value in enumerate(carry):
                totals[at] += value

            @pl.when(has_outer)
            def _():
                to_outer(k, d, rx, c).start()

        for at in range(sums):
            totals[at] = zero

        @pl.loop(0, chunks + lag)
        def _(step):
            @pl.when(step < chunks)
            def _():
                inbound(step)

            @pl.when(step >= lag)
            def _():
                outbound(step - lag)

    def term_copy(s, msg, trx, k):
        return pltpu.make_async_remote_copy(
            src_ref=msg.at[k], dst_ref=trx.at[k],
            send_sem=t_send.at[s, k], recv_sem=t_recv.at[s, k],
            device_id={"term": partner_of(k)}, device_id_type=MESH,
        )

    def term_sum(s, msg, trx):
        for k in range(rounds):
            copy = term_copy(s, msg, trx, k)
            copy.start()
            copy.wait()
            msg[k + 1] = msg[k] + trx[k]

    def sq_copy(s, sq, sr, off):
        return pltpu.make_async_remote_copy(
            src_ref=sq, dst_ref=sr.at[me],
            send_sem=s_send.at[s, off], recv_sem=s_recv.at[s, off],
            device_id={"samp": peer_of(off)}, device_id_type=MESH,
        )

    def samp_start(s, sq, sr):
        @pl.loop(1, n_samp)
        def _(off):
            sq_copy(s, sq, sr, off).start()

        sr[me] = sq[...]

    def samp_finish(s, sq, sr):
        @pl.loop(1, n_samp)
        def _(off):
            sq_copy(s, sq, sr, off).wait()

        total = lax.fori_loop(1, n_samp, lambda i, t: t + sr[i], sr[0])
        return lane_sum(total)

    lane = lax.broadcasted_iota(jnp.int32, (num_out, width), 1)

    def pack(values):
        out = jnp.zeros((num_out, width), F32)
        for at, v in enumerate(values):
            out = jnp.where(lane == at, lane_sum(v), out)
        return out

    def pick(block, at):
        return lane_sum(jnp.where(lane == at, block, 0.0))

    def damp_sq(b):
        d = 0.4 * (1.0 + deg[b].astype(F32))
        return d * d

    adjoint(lambda r: t_ref[:, pl.ds(pl.multiple_of(r * width, width), width)], True)
    pl.semaphore_wait(barrier, n_samp - 1 + rounds)

    def visit0(b, v, carry):
        gs, os = carry
        sq = v * v
        return gs + sq, os + damp_sq(b) * sq

    chain(0, acc0, rx0, d0, visit0, 2)
    forward(d0, msg0)
    msg0[0, rows] = pack([totals[0], totals[1]])
    term_sum(0, msg0, trx0)
    scal = msg0[rounds, rows]
    gsq0, own0 = pick(scal, 0), pick(scal, 1)

    sq = zero
    for r in range(rows):
        v = msg0[rounds, r]
        img0[r] = v
        sq = sq + v * v
    sq0[...] = sq
    samp_start(0, sq0, sr0)
    adjoint(lambda r: img0[r], False)
    chain(1, acc1, rx1, w1, lambda b, v, c: c, 0)
    alpha0 = gsq0 / (samp_finish(0, sq0, sr0) + own0)
    alpha0 = jnp.broadcast_to(alpha0, (num_out, width))

    def make_grad(b, carry):
        ns, s1, s2 = carry
        dd = damp_sq(b)
        d = d0[b]
        g = d - alpha0 * (w1[b] + dd * d)
        g1[b] = g
        dg = dd * g
        return ns + g * g, s1 + dg * g, s2 + dg * d

    ns, s1, s2 = lax.fori_loop(0, terms, make_grad, (zero, zero, zero))
    forward(g1, msg1)
    msg1[0, rows] = pack([ns, s1, s2])
    term_sum(1, msg1, trx1)
    scal = msg1[rounds, rows]
    gsq1, c1, c2 = pick(scal, 0), pick(scal, 1), pick(scal, 2)
    beta = gsq1 / gsq0
    own1 = c1 + 2.0 * beta * c2 + beta * beta * own0
    beta = jnp.broadcast_to(beta, (num_out, width))

    sq = zero
    for r in range(rows):
        v = msg1[rounds, r] + beta * img0[r]
        img1[r] = v
        sq = sq + v * v
    sq1[...] = sq
    samp_start(1, sq1, sr1)
    alpha1 = gsq1 / (samp_finish(1, sq1, sr1) + own1)
    alpha1 = jnp.broadcast_to(alpha1, (num_out, width))
    both = alpha0 + alpha1 * beta

    @pl.loop(0, terms)
    def _(b):
        sol_ref[:, pl.ds(pl.multiple_of(b * width, width), width)] = both * d0[b] + alpha1 * g1[b]

    for r in range(rows):
        cols = slice(r * width, (r + 1) * width)
        res_ref[:, cols] = t_ref[:, cols] - alpha0 * img0[r] - alpha1 * img1[r]

    for k, (acc, rx, d) in enumerate(((acc0, rx0, d0), (acc1, rx1, w1))):
        @pl.loop(0, chunks)
        def _(c):
            to_inner(k, acc, rx, c).wait_send()

            @pl.when(has_outer)
            def _():
                to_outer(k, d, rx, c).wait_send()


def local(n_samp, n_term, blocks, term_index, degrees, targets):
    rows, touched, width = blocks.shape[2], blocks.shape[3], blocks.shape[4]
    terms = degrees.shape[0]
    num_out = targets.shape[0]
    pattern = term_index[0, 0]
    hit = pattern[:, :, None] == jnp.arange(terms, dtype=jnp.int32)
    at = jnp.arange(touched, dtype=jnp.int32)[None, :, None]
    where = jnp.min(jnp.where(hit, at, touched), axis=1)
    where = where + jnp.arange(rows, dtype=jnp.int32)[:, None] * (touched + 1)
    tab = jnp.concatenate([where, pattern], axis=1)

    chunks = min(16, terms)
    rounds = n_term.bit_length() - 1
    blk = (num_out, width)
    vmem = pl.BlockSpec(memory_space=pltpu.VMEM)
    smem = pl.BlockSpec(memory_space=pltpu.SMEM)
    V = pltpu.VMEM
    dma = pltpu.SemaphoreType.DMA
    return pl.pallas_call(
        functools.partial(kernel, n_samp, n_term, chunks),
        out_shape=(
            jax.ShapeDtypeStruct((num_out, terms * width), F32),
            jax.ShapeDtypeStruct((num_out, rows * width), F32),
        ),
        in_specs=[smem, smem, vmem, vmem],
        out_specs=(vmem, vmem),
        scratch_shapes=[
            V((rows, width, touched * width), BF16),
            V((rows, width, touched * width), BF16),
            V((rows * (touched + 1),) + blk, F32),
            V((terms,) + blk, F32),
            V((terms,) + blk, F32),
            V((2, terms) + blk, F32),
            V((2, terms) + blk, F32),
            V((terms,) + blk, F32),
            V((terms,) + blk, F32),
            V((terms,) + blk, F32),
            V((rows,) + blk, F32),
            V((rows,) + blk, F32),
            V((rounds + 1, rows + 1) + blk, F32),
            V((rounds + 1, rows + 1) + blk, F32),
            V((rounds, rows + 1) + blk, F32),
            V((rounds, rows + 1) + blk, F32),
            V((n_samp,) + blk, F32),
            V((n_samp,) + blk, F32),
            V(blk, F32),
            V(blk, F32),
            V((2,) + blk, F32),
            dma((2, chunks)),
            dma((2, chunks)),
            dma((2, 2, chunks)),
            dma((2, rounds)),
            dma((2, rounds)),
            dma((2, n_samp)),
            dma((2, n_samp)),
        ],
        compiler_params=pltpu.CompilerParams(
            collective_id=0, has_side_effects=True, vmem_limit_bytes=48 * 1024 * 1024,
        ),
    )(tab, degrees, blocks, targets)


def solution(mesh):
    placed = (
        P("samp", "term", "grp", None, None, None),
        P("samp", "term", "grp", None),
        P("term"),
        P("grp", "samp"),
    )
    return jax.shard_map(
        functools.partial(local, mesh.shape["samp"], mesh.shape["term"]),
        mesh=mesh,
        in_specs=placed,
        out_specs=(P("grp", "term"), P("grp", "samp")),
        check_vma=False,
    )
```

```python
import functools

import jax
import jax.numpy as jnp
from jax import lax
from jax.experimental import pallas as pl
from jax.experimental.pallas import tpu as pltpu
from jax.sharding import PartitionSpec as P

MESH = pl.DeviceIdType.MESH
F32 = jnp.float32
BF16 = jnp.bfloat16
LAG = 4
LAG_MID = 2
PIECES = 3


def split(x):
    hi = x.astype(BF16)
    return hi, (x - hi.astype(F32)).astype(BF16)


def lane_sum(x):
    return jnp.sum(x, axis=1, keepdims=True)


def kernel(
    n_samp, n_term, chunks,
    idx_ref, deg, a_hbm, t_ref,
    sol_ref, res_ref,
    tab, tab_v, tab_sem, a_ref, a_sem, ahi, alo, part, acc0, acc1, rx0, rx1, d0, w1, g1,
    img0, img1, msg0, msg1, trx0, trx1, sr0, sr1, sq0, sq1, totals,
    in_send, out_send, chain_recv, t_send, t_recv, s_send, s_recv,
):
    rows, touched, width = a_ref.shape[0], a_ref.shape[1], a_ref.shape[2]
    num_out = t_ref.shape[0]
    terms = deg.shape[0]
    size = terms // chunks
    half = n_samp // 2
    rounds = n_term.bit_length() - 1
    cuts = [(rows + 1) * p // PIECES for p in range(PIECES + 1)]
    me = lax.axis_index("samp")
    tm = lax.axis_index("term")

    low = me < half
    inner = jnp.where(low, me + 1, me - 1)
    is_mid = jnp.logical_or(me == half - 1, me == half)
    has_outer = jnp.logical_and(me > 0, me < n_samp - 1)
    outer = jnp.where(low, jnp.maximum(me - 1, 0), jnp.minimum(me + 1, n_samp - 1))
    away = jnp.where(low, half - 1 - me, me - half)
    lag = jnp.minimum(LAG * 2 * away + LAG_MID, chunks)
    slot_at_inner = jnp.where(is_mid, 1, 0)

    zero = jnp.zeros((num_out, width), F32)

    def peer_of(off):
        return lax.rem(me + off, n_samp)

    def partner_of(k):
        step = 2 ** k
        return tm + (1 - 2 * lax.rem(tm // step, 2)) * step

    def block_copy(r):
        return pltpu.make_async_copy(a_hbm.at[0, 0, r], a_ref.at[r], a_sem.at[r])

    @pl.loop(0, rows)
    def _(r):
        block_copy(r).start()

    barrier = pltpu.get_barrier_semaphore()

    @pl.loop(1, n_samp)
    def _(off):
        pl.semaphore_signal(barrier, inc=1, device_id={"samp": peer_of(off)}, device_id_type=MESH)

    for k in range(rounds):
        pl.semaphore_signal(barrier, inc=1, device_id={"term": partner_of(k)}, device_id_type=MESH)

    pattern = idx_ref[0, 0]
    shape = tab_v.shape
    term = lax.broadcasted_iota(jnp.int32, shape, 1)
    none = lax.broadcasted_iota(jnp.int32, shape, 0) * (touched + 1) + touched
    table = none
    for n in range(touched):
        col = pattern[:, n:n + 1]
        table = jnp.where(term == col, none + (n - touched), table)
        table = jnp.where(term == terms + n, col, table)
    tab_v[...] = table
    tab_copy = pltpu.make_async_copy(tab_v, tab, tab_sem)
    tab_copy.start()

    def adjoint(load, first):
        @pl.loop(0, rows)
        def _(r):
            if first:
                block_copy(r).wait()
                for n in range(touched):
                    hi, lo = split(a_ref[r, n])
                    ahi[r, :, n * width:(n + 1) * width] = hi
                    alo[r, :, n * width:(n + 1) * width] = lo
                part[r * (touched + 1) + touched] = jnp.zeros((num_out, width), F32)
            hi, lo = split(load(r))
            both = jnp.concatenate([hi, lo], axis=0)
            for n in range(touched):
                cols = slice(n * width, (n + 1) * width)
                p = jnp.dot(both, ahi[r, :, cols], preferred_element_type=F32)
                q = jnp.dot(hi, alo[r, :, cols], preferred_element_type=F32)
                part[r * (touched + 1) + n] = p[:num_out] + p[num_out:] + q

    def forward(src, dst, start, stop):
        @pl.loop(start, stop)
        def _(r):
            x = jnp.concatenate([src[tab[r, terms + n]] for n in range(touched)], axis=1)
            hi, lo = split(x)
            both = jnp.concatenate([hi, lo], axis=0)
            dims = (((1,), (1,)), ((), ()))
            p = lax.dot_general(both, ahi[r], dims, preferred_element_type=F32)
            q = lax.dot_general(hi, alo[r], dims, preferred_element_type=F32)
            dst[0, r] = p[:num_out] + p[num_out:] + q

    def span(c):
        return pl.ds(c * size, size)

    def to_inner(k, acc, rx, c):
        return pltpu.make_async_remote_copy(
            src_ref=acc.at[span(c)], dst_ref=rx.at[slot_at_inner, span(c)],
            send_sem=in_send.at[k, c], recv_sem=chain_recv.at[k, slot_at_inner, c],
            device_id={"samp": inner}, device_id_type=MESH,
        )

    def to_outer(k, d, rx, c):
        return pltpu.make_async_remote_copy(
            src_ref=d.at[span(c)], dst_ref=rx.at[1, span(c)],
            send_sem=out_send.at[k, c], recv_sem=chain_recv.at[k, 1, c],
            device_id={"samp": outer}, device_id_type=MESH,
        )

    def arrived(k, rx, slot, c):
        pltpu.make_async_remote_copy(
            src_ref=rx.at[slot, span(c)], dst_ref=rx.at[slot, span(c)],
            send_sem=in_send.at[k, c], recv_sem=chain_recv.at[k, slot, c],
            device_id={"samp": inner}, device_id_type=MESH,
        ).wait_recv()

    def chain(k, acc, rx, d, visit, sums):
        def inbound(c):
            @pl.loop(0, size, unroll=True)
            def _(i):
                b = c * size + i
                total = part[tab[0, b]]
                for r in range(1, rows):
                    total = total + part[tab[r, b]]
                acc[b] = total

            @pl.when(has_outer)
            def _():
                arrived(k, rx, 0, c)
                acc[span(c)] += rx[0, span(c)]

            to_inner(k, acc, rx, c).start()

        def outbound(c):
            arrived(k, rx, 1, c)

            def one(i, carry):
                b = c * size + i
                got = rx[1, b]
                v = jnp.where(is_mid, got + acc[b], got)
                d[b] = v
                return visit(b, v, carry)

            carry = lax.fori_loop(0, size, one, tuple(zero for _ in range(sums)), unroll=True)
            for at, value in enumerate(carry):
                totals[at] += value

            @pl.when(has_outer)
            def _():
                to_outer(k, d, rx, c).start()

        for at in range(sums):
            totals[at] = zero

        @pl.loop(0, chunks + lag)
        def _(step):
            @pl.when(step < chunks)
            def _():
                inbound(step)

            @pl.when(step >= lag)
            def _():
                outbound(step - lag)

    def term_copy(s, msg, trx, k, p):
        part_of = pl.ds(cuts[p], cuts[p + 1] - cuts[p])
        return pltpu.make_async_remote_copy(
            src_ref=msg.at[k, part_of], dst_ref=trx.at[k, part_of],
            send_sem=t_send.at[s, k, p], recv_sem=t_recv.at[s, k, p],
            device_id={"term": partner_of(k)}, device_id_type=MESH,
        )

    def image_sum(s, src, msg, trx, scalars):
        def advance(k, p):
            term_copy(s, msg, trx, k, p).wait()
            part_of = pl.ds(cuts[p], cuts[p + 1] - cuts[p])
            msg[k + 1, part_of] = msg[k, part_of] + trx[k, part_of]
            if k + 1 < rounds:
                term_copy(s, msg, trx, k + 1, p).start()

        msg[0, rows] = pack(scalars)
        for p in range(PIECES):
            forward(src, msg, cuts[p], min(cuts[p + 1], rows))
            term_copy(s, msg, trx, 0, p).start()
            if p:
                advance(0, p - 1)
        advance(0, PIECES - 1)
        for k in range(1, rounds):
            for p in range(PIECES):
                advance(k, p)

    def sq_copy(s, sq, sr, off):
        return pltpu.make_async_remote_copy(
            src_ref=sq, dst_ref=sr.at[me],
            send_sem=s_send.at[s, off], recv_sem=s_recv.at[s, off],
            device_id={"samp": peer_of(off)}, device_id_type=MESH,
        )

    def samp_start(s, sq, sr):
        @pl.loop(1, n_samp)
        def _(off):
            sq_copy(s, sq, sr, off).start()

        sr[me] = sq[...]

    def samp_finish(s, sq, sr):
        @pl.loop(1, n_samp)
        def _(off):
            sq_copy(s, sq, sr, off).wait()

        total = lax.fori_loop(1, n_samp, lambda i, t: t + sr[i], sr[0])
        return lane_sum(total)

    lane = lax.broadcasted_iota(jnp.int32, (num_out, width), 1)

    def pack(values):
        out = jnp.zeros((num_out, width), F32)
        for at, v in enumerate(values):
            out = jnp.where(lane == at, lane_sum(v), out)
        return out

    def pick(block, at):
        return lane_sum(jnp.where(lane == at, block, 0.0))

    def damp_sq(b):
        d = 0.4 * (1.0 + deg[b].astype(F32))
        return d * d

    adjoint(lambda r: t_ref[:, pl.ds(pl.multiple_of(r * width, width), width)], True)
    tab_copy.wait()
    pl.semaphore_wait(barrier, n_samp - 1 + rounds)

    def visit0(b, v, carry):
        gs, os = carry
        sq = v * v
        return gs + sq, os + damp_sq(b) * sq

    chain(0, acc0, rx0, d0, visit0, 2)
    image_sum(0, d0, msg0, trx0, [totals[0], totals[1]])
    scal = msg0[rounds, rows]
    gsq0, own0 = pick(scal, 0), pick(scal, 1)

    sq = zero
    for r in range(rows):
        v = msg0[rounds, r]
        img0[r] = v
        sq = sq + v * v
    sq0[...] = sq
    samp_start(0, sq0, sr0)
    adjoint(lambda r: img0[r], False)
    chain(1, acc1, rx1, w1, lambda b, v, c: c, 0)
    alpha0 = gsq0 / (samp_finish(0, sq0, sr0) + own0)
    alpha0 = jnp.broadcast_to(alpha0, (num_out, width))

    def make_grad(b, carry):
        ns, s1, s2 = carry
        dd = damp_sq(b)
        d = d0[b]
        g = d - alpha0 * (w1[b] + dd * d)
        g1[b] = g
        dg = dd * g
        return ns + g * g, s1 + dg * g, s2 + dg * d

    ns, s1, s2 = lax.fori_loop(0, terms, make_grad, (zero, zero, zero), unroll=4)
    image_sum(1, g1, msg1, trx1, [ns, s1, s2])
    scal = msg1[rounds, rows]
    gsq1, c1, c2 = pick(scal, 0), pick(scal, 1), pick(scal, 2)
    beta = gsq1 / gsq0
    own1 = c1 + 2.0 * beta * c2 + beta * beta * own0
    beta = jnp.broadcast_to(beta, (num_out, width))

    sq = zero
    for r in range(rows):
        v = msg1[rounds, r] + beta * img0[r]
        img1[r] = v
        sq = sq + v * v
    sq1[...] = sq
    samp_start(1, sq1, sr1)
    alpha1 = gsq1 / (samp_finish(1, sq1, sr1) + own1)
    alpha1 = jnp.broadcast_to(alpha1, (num_out, width))
    both = alpha0 + alpha1 * beta

    @pl.loop(0, terms, unroll=4)
    def _(b):
        sol_ref[:, pl.ds(pl.multiple_of(b * width, width), width)] = both * d0[b] + alpha1 * g1[b]

    for r in range(rows):
        cols = slice(r * width, (r + 1) * width)
        res_ref[:, cols] = t_ref[:, cols] - alpha0 * img0[r] - alpha1 * img1[r]

    for k, (acc, rx, d) in enumerate(((acc0, rx0, d0), (acc1, rx1, w1))):
        @pl.loop(0, chunks)
        def _(c):
            to_inner(k, acc, rx, c).wait_send()

            @pl.when(has_outer)
            def _():
                to_outer(k, d, rx, c).wait_send()


def local(n_samp, n_term, blocks, term_index, degrees, targets):
    rows, touched, width = blocks.shape[2], blocks.shape[3], blocks.shape[4]
    terms = degrees.shape[0]
    num_out = targets.shape[0]
    chunks = min(16, terms)
    rounds = n_term.bit_length() - 1
    blk = (num_out, width)
    tab_cols = -(-(terms + touched) // 128) * 128
    vmem = pl.BlockSpec(memory_space=pltpu.VMEM)
    smem = pl.BlockSpec(memory_space=pltpu.SMEM)
    V = pltpu.VMEM
    dma = pltpu.SemaphoreType.DMA
    return pl.pallas_call(
        functools.partial(kernel, n_samp, n_term, chunks),
        out_shape=(
            jax.ShapeDtypeStruct((num_out, terms * width), F32),
            jax.ShapeDtypeStruct((num_out, rows * width), F32),
        ),
        in_specs=[vmem, smem, pl.BlockSpec(memory_space=pltpu.HBM), vmem],
        out_specs=(vmem, vmem),
        scratch_shapes=[
            pltpu.SMEM((rows, tab_cols), jnp.int32),
            V((rows, tab_cols), jnp.int32),
            dma,
            V((rows, touched, width, width), F32),
            dma((rows,)),
            V((rows, width, touched * width), BF16),
            V((rows, width, touched * width), BF16),
            V((rows * (touched + 1),) + blk, F32),
            V((terms,) + blk, F32),
            V((terms,) + blk, F32),
            V((2, terms) + blk, F32),
            V((2, terms) + blk, F32),
            V((terms,) + blk, F32),
            V((terms,) + blk, F32),
            V((terms,) + blk, F32),
            V((rows,) + blk, F32),
            V((rows,) + blk, F32),
            V((rounds + 1, rows + 1) + blk, F32),
            V((rounds + 1, rows + 1) + blk, F32),
            V((rounds, rows + 1) + blk, F32),
            V((rounds, rows + 1) + blk, F32),
            V((n_samp,) + blk, F32),
            V((n_samp,) + blk, F32),
            V(blk, F32),
            V(blk, F32),
            V((2,) + blk, F32),
            dma((2, chunks)),
            dma((2, chunks)),
            dma((2, 2, chunks)),
            dma((2, rounds, PIECES)),
            dma((2, rounds, PIECES)),
            dma((2, n_samp)),
            dma((2, n_samp)),
        ],
        compiler_params=pltpu.CompilerParams(
            collective_id=0, has_side_effects=True, vmem_limit_bytes=48 * 1024 * 1024,
        ),
    )(term_index, degrees, blocks, targets)


def solution(mesh):
    placed = (
        P("samp", "term", "grp", None, None, None),
        P("samp", "term", "grp", None),
        P("term"),
        P("grp", "samp"),
    )
    return jax.shard_map(
        functools.partial(local, mesh.shape["samp"], mesh.shape["term"]),
        mesh=mesh,
        in_specs=placed,
        out_specs=(P("grp", "term"), P("grp", "samp")),
        check_vma=False,
    )
```

```python
import functools

import jax
import jax.numpy as jnp
from jax import lax
from jax.experimental import pallas as pl
from jax.experimental.pallas import tpu as pltpu
from jax.sharding import PartitionSpec as P

MESH = pl.DeviceIdType.MESH
F32 = jnp.float32
BF16 = jnp.bfloat16
LAG = 4
LAG_MID = 2
PIECES = 3


def split(x):
    hi = x.astype(BF16)
    return hi, (x - hi.astype(F32)).astype(BF16)


def lane_sum(x):
    return jnp.sum(x, axis=1, keepdims=True)


def kernel(
    n_samp, n_term, chunks,
    idx_ref, deg, a_hbm, t_ref,
    sol_ref, res_ref,
    tab, tab_v, tab_sem, a_ref, a_sem, ahi, alo, part, acc0, acc1, rx0, rx1, d0, w1, g1,
    img0, img1, msg0, msg1, trx0, trx1, sr0, sr1, sq0, sq1, totals,
    in_send, out_send, chain_recv, t_send, t_recv, s_send, s_recv,
):
    rows, touched, width = a_ref.shape[0], a_ref.shape[1], a_ref.shape[2]
    num_out = t_ref.shape[0]
    terms = deg.shape[0]
    size = terms // chunks
    half = n_samp // 2
    rounds = n_term.bit_length() - 1
    cuts = [(rows + 1) * p // PIECES for p in range(PIECES + 1)]
    me = lax.axis_index("samp")
    tm = lax.axis_index("term")

    low = me < half
    inner = jnp.where(low, me + 1, me - 1)
    is_mid = jnp.logical_or(me == half - 1, me == half)
    has_outer = jnp.logical_and(me > 0, me < n_samp - 1)
    outer = jnp.where(low, jnp.maximum(me - 1, 0), jnp.minimum(me + 1, n_samp - 1))
    away = jnp.where(low, half - 1 - me, me - half)
    lag = jnp.minimum(LAG * 2 * away + LAG_MID, chunks)
    slot_at_inner = jnp.where(is_mid, 1, 0)

    zero = jnp.zeros((num_out, width), F32)

    def peer_of(off):
        return lax.rem(me + off, n_samp)

    def partner_of(k):
        step = 2 ** k
        return tm + (1 - 2 * lax.rem(tm // step, 2)) * step

    def block_copy(r):
        return pltpu.make_async_copy(a_hbm.at[0, 0, r], a_ref.at[r], a_sem.at[r])

    @pl.loop(0, rows)
    def _(r):
        block_copy(r).start()

    barrier = pltpu.get_barrier_semaphore()

    @pl.loop(1, n_samp)
    def _(off):
        pl.semaphore_signal(barrier, inc=1, device_id={"samp": peer_of(off)}, device_id_type=MESH)

    for k in range(rounds):
        pl.semaphore_signal(barrier, inc=1, device_id={"term": partner_of(k)}, device_id_type=MESH)

    pattern = idx_ref[0, 0]
    shape = tab_v.shape
    term = lax.broadcasted_iota(jnp.int32, shape, 1)
    none = lax.broadcasted_iota(jnp.int32, shape, 0) * (touched + 1) + touched
    table = none
    for n in range(touched):
        col = pattern[:, n:n + 1]
        table = jnp.where(term == col, none + (n - touched), table)
        table = jnp.where(term == terms + n, col, table)
    tab_v[...] = table
    tab_copy = pltpu.make_async_copy(tab_v, tab, tab_sem)
    tab_copy.start()

    def adjoint(load, first):
        @pl.loop(0, rows, unroll=2)
        def _(r):
            if first:
                block_copy(r).wait()
                for n in range(touched):
                    hi, lo = split(a_ref[r, n])
                    ahi[r, :, n * width:(n + 1) * width] = hi
                    alo[r, :, n * width:(n + 1) * width] = lo
                part[r * (touched + 1) + touched] = jnp.zeros((num_out, width), F32)
            hi, lo = split(load(r))
            both = jnp.concatenate([hi, lo], axis=0)
            for n in range(touched):
                cols = slice(n * width, (n + 1) * width)
                p = jnp.dot(both, ahi[r, :, cols], preferred_element_type=F32)
                q = jnp.dot(hi, alo[r, :, cols], preferred_element_type=F32)
                part[r * (touched + 1) + n] = p[:num_out] + p[num_out:] + q

    def forward(src, dst, start, stop):
        @pl.loop(start, stop, unroll=True)
        def _(r):
            x = jnp.concatenate([src[tab[r, terms + n]] for n in range(touched)], axis=1)
            hi, lo = split(x)
            both = jnp.concatenate([hi, lo], axis=0)
            dims = (((1,), (1,)), ((), ()))
            p = lax.dot_general(both, ahi[r], dims, preferred_element_type=F32)
            q = lax.dot_general(hi, alo[r], dims, preferred_element_type=F32)
            dst[0, r] = p[:num_out] + p[num_out:] + q

    def span(c):
        return pl.ds(c * size, size)

    def to_inner(k, acc, rx, c):
        return pltpu.make_async_remote_copy(
            src_ref=acc.at[span(c)], dst_ref=rx.at[slot_at_inner, span(c)],
            send_sem=in_send.at[k, c], recv_sem=chain_recv.at[k, slot_at_inner, c],
            device_id={"samp": inner}, device_id_type=MESH,
        )

    def to_outer(k, d, rx, c):
        return pltpu.make_async_remote_copy(
            src_ref=d.at[span(c)], dst_ref=rx.at[1, span(c)],
            send_sem=out_send.at[k, c], recv_sem=chain_recv.at[k, 1, c],
            device_id={"samp": outer}, device_id_type=MESH,
        )

    def arrived(k, rx, slot, c):
        pltpu.make_async_remote_copy(
            src_ref=rx.at[slot, span(c)], dst_ref=rx.at[slot, span(c)],
            send_sem=in_send.at[k, c], recv_sem=chain_recv.at[k, slot, c],
            device_id={"samp": inner}, device_id_type=MESH,
        ).wait_recv()

    def chain(k, acc, rx, d, visit, sums):
        def inbound(c):
            @pl.loop(0, size, unroll=True)
            def _(i):
                b = c * size + i
                total = part[tab[0, b]]
                for r in range(1, rows):
                    total = total + part[tab[r, b]]
                acc[b] = total

            @pl.when(has_outer)
            def _():
                arrived(k, rx, 0, c)
                acc[span(c)] += rx[0, span(c)]

            to_inner(k, acc, rx, c).start()

        def outbound(c):
            arrived(k, rx, 1, c)

            @pl.loop(0, size, unroll=True)
            def _(i):
                b = c * size + i
                got = rx[1, b]
                d[b] = jnp.where(is_mid, got + acc[b], got)

            @pl.when(has_outer)
            def _():
                to_outer(k, d, rx, c).start()

            def one(i, carry):
                b = c * size + i
                return visit(b, d[b], carry)

            carry = lax.fori_loop(0, size, one, tuple(zero for _ in range(sums)), unroll=True)
            for at, value in enumerate(carry):
                totals[at] += value

        for at in range(sums):
            totals[at] = zero

        @pl.loop(0, chunks + lag)
        def _(step):
            @pl.when(step < chunks)
            def _():
                inbound(step)

            @pl.when(step >= lag)
            def _():
                outbound(step - lag)

    def term_copy(s, msg, trx, k, p):
        part_of = pl.ds(cuts[p], cuts[p + 1] - cuts[p])
        return pltpu.make_async_remote_copy(
            src_ref=msg.at[k, part_of], dst_ref=trx.at[k, part_of],
            send_sem=t_send.at[s, k, p], recv_sem=t_recv.at[s, k, p],
            device_id={"term": partner_of(k)}, device_id_type=MESH,
        )

    def image_sum(s, src, msg, trx, scalars):
        def advance(k, p):
            term_copy(s, msg, trx, k, p).wait()
            part_of = pl.ds(cuts[p], cuts[p + 1] - cuts[p])
            msg[k + 1, part_of] = msg[k, part_of] + trx[k, part_of]
            if k + 1 < rounds:
                term_copy(s, msg, trx, k + 1, p).start()

        msg[0, rows] = pack(scalars)
        for p in range(PIECES):
            forward(src, msg, cuts[p], min(cuts[p + 1], rows))
            term_copy(s, msg, trx, 0, p).start()
            if p:
                advance(0, p - 1)
        advance(0, PIECES - 1)
        for k in range(1, rounds):
            for p in range(PIECES):
                advance(k, p)

    def sq_copy(s, sq, sr, off):
        return pltpu.make_async_remote_copy(
            src_ref=sq, dst_ref=sr.at[me],
            send_sem=s_send.at[s, off], recv_sem=s_recv.at[s, off],
            device_id={"samp": peer_of(off)}, device_id_type=MESH,
        )

    def samp_start(s, sq, sr):
        @pl.loop(1, n_samp)
        def _(off):
            sq_copy(s, sq, sr, off).start()

        sr[me] = sq[...]

    def samp_finish(s, sq, sr):
        @pl.loop(1, n_samp)
        def _(off):
            sq_copy(s, sq, sr, off).wait()

        total = lax.fori_loop(1, n_samp, lambda i, t: t + sr[i], sr[0])
        return lane_sum(total)

    lane = lax.broadcasted_iota(jnp.int32, (num_out, width), 1)

    def pack(values):
        out = jnp.zeros((num_out, width), F32)
        for at, v in enumerate(values):
            out = jnp.where(lane == at, lane_sum(v), out)
        return out

    def pick(block, at):
        return lane_sum(jnp.where(lane == at, block, 0.0))

    def damp_sq(b):
        d = 0.4 * (1.0 + deg[b].astype(F32))
        return d * d

    adjoint(lambda r: t_ref[:, pl.ds(pl.multiple_of(r * width, width), width)], True)
    tab_copy.wait()
    pl.semaphore_wait(barrier, n_samp - 1 + rounds)

    def visit0(b, v, carry):
        gs, os = carry
        sq = v * v
        return gs + sq, os + damp_sq(b) * sq

    chain(0, acc0, rx0, d0, visit0, 2)
    image_sum(0, d0, msg0, trx0, [totals[0], totals[1]])
    scal = msg0[rounds, rows]
    gsq0, own0 = pick(scal, 0), pick(scal, 1)

    sq = zero
    for r in range(rows):
        v = msg0[rounds, r]
        img0[r] = v
        sq = sq + v * v
    sq0[...] = sq
    samp_start(0, sq0, sr0)
    adjoint(lambda r: img0[r], False)
    chain(1, acc1, rx1, w1, lambda b, v, c: c, 0)
    alpha0 = gsq0 / (samp_finish(0, sq0, sr0) + own0)
    alpha0 = jnp.broadcast_to(alpha0, (num_out, width))

    def make_grad(b, carry):
        ns, s1, s2 = carry
        dd = damp_sq(b)
        d = d0[b]
        g = d - alpha0 * (w1[b] + dd * d)
        g1[b] = g
        dg = dd * g
        return ns + g * g, s1 + dg * g, s2 + dg * d

    ns, s1, s2 = lax.fori_loop(0, terms, make_grad, (zero, zero, zero), unroll=4)
    image_sum(1, g1, msg1, trx1, [ns, s1, s2])
    scal = msg1[rounds, rows]
    gsq1, c1, c2 = pick(scal, 0), pick(scal, 1), pick(scal, 2)
    beta = gsq1 / gsq0
    own1 = c1 + 2.0 * beta * c2 + beta * beta * own0
    beta = jnp.broadcast_to(beta, (num_out, width))

    sq = zero
    for r in range(rows):
        v = msg1[rounds, r] + beta * img0[r]
        img1[r] = v
        sq = sq + v * v
    sq1[...] = sq
    samp_start(1, sq1, sr1)
    alpha1 = gsq1 / (samp_finish(1, sq1, sr1) + own1)
    alpha1 = jnp.broadcast_to(alpha1, (num_out, width))
    both = alpha0 + alpha1 * beta

    @pl.loop(0, terms, unroll=4)
    def _(b):
        sol_ref[:, pl.ds(pl.multiple_of(b * width, width), width)] = both * d0[b] + alpha1 * g1[b]

    for r in range(rows):
        cols = slice(r * width, (r + 1) * width)
        res_ref[:, cols] = t_ref[:, cols] - alpha0 * img0[r] - alpha1 * img1[r]

    for k, (acc, rx, d) in enumerate(((acc0, rx0, d0), (acc1, rx1, w1))):
        @pl.loop(0, chunks)
        def _(c):
            to_inner(k, acc, rx, c).wait_send()

            @pl.when(has_outer)
            def _():
                to_outer(k, d, rx, c).wait_send()


def local(n_samp, n_term, blocks, term_index, degrees, targets):
    rows, touched, width = blocks.shape[2], blocks.shape[3], blocks.shape[4]
    terms = degrees.shape[0]
    num_out = targets.shape[0]
    chunks = min(16, terms)
    rounds = n_term.bit_length() - 1
    blk = (num_out, width)
    tab_cols = -(-(terms + touched) // 128) * 128
    vmem = pl.BlockSpec(memory_space=pltpu.VMEM)
    smem = pl.BlockSpec(memory_space=pltpu.SMEM)
    V = pltpu.VMEM
    dma = pltpu.SemaphoreType.DMA
    return pl.pallas_call(
        functools.partial(kernel, n_samp, n_term, chunks),
        out_shape=(
            jax.ShapeDtypeStruct((num_out, terms * width), F32),
            jax.ShapeDtypeStruct((num_out, rows * width), F32),
        ),
        in_specs=[vmem, smem, pl.BlockSpec(memory_space=pltpu.HBM), vmem],
        out_specs=(vmem, vmem),
        scratch_shapes=[
            pltpu.SMEM((rows, tab_cols), jnp.int32),
            V((rows, tab_cols), jnp.int32),
            dma,
            V((rows, touched, width, width), F32),
            dma((rows,)),
            V((rows, width, touched * width), BF16),
            V((rows, width, touched * width), BF16),
            V((rows * (touched + 1),) + blk, F32),
            V((terms,) + blk, F32),
            V((terms,) + blk, F32),
            V((2, terms) + blk, F32),
            V((2, terms) + blk, F32),
            V((terms,) + blk, F32),
            V((terms,) + blk, F32),
            V((terms,) + blk, F32),
            V((rows,) + blk, F32),
            V((rows,) + blk, F32),
            V((rounds + 1, rows + 1) + blk, F32),
            V((rounds + 1, rows + 1) + blk, F32),
            V((rounds, rows + 1) + blk, F32),
            V((rounds, rows + 1) + blk, F32),
            V((n_samp,) + blk, F32),
            V((n_samp,) + blk, F32),
            V(blk, F32),
            V(blk, F32),
            V((2,) + blk, F32),
            dma((2, chunks)),
            dma((2, chunks)),
            dma((2, 2, chunks)),
            dma((2, rounds, PIECES)),
            dma((2, rounds, PIECES)),
            dma((2, n_samp)),
            dma((2, n_samp)),
        ],
        compiler_params=pltpu.CompilerParams(
            collective_id=0, has_side_effects=True, vmem_limit_bytes=48 * 1024 * 1024,
        ),
    )(term_index, degrees, blocks, targets)


def solution(mesh):
    placed = (
        P("samp", "term", "grp", None, None, None),
        P("samp", "term", "grp", None),
        P("term"),
        P("grp", "samp"),
    )
    return jax.shard_map(
        functools.partial(local, mesh.shape["samp"], mesh.shape["term"]),
        mesh=mesh,
        in_specs=placed,
        out_specs=(P("grp", "term"), P("grp", "samp")),
        check_vma=False,
    )
```
